256 devices in a mesh: outer: 16 (over z_lo, x), inner: 16 (over z_hi, y, core).
Axes of the slice: x: 4, y: 4, z: 8 (z_hi: 2, z_lo: 4; z = z_hi * 4 + z_lo), core: 2. Of those that a mesh axis runs over, the one named last changes fastest.
Arguments:
- queries: bfloat16 [262144, 128], P(('outer', 'inner')), may hold values from -6 to 6
- key_block: bfloat16 [262144, 128], P(('outer', 'inner')), may hold values from -6 to 6
- value_block: bfloat16 [262144, 128], P(('outer', 'inner')), may hold values from -6 to 6
- out_grad: bfloat16 [262144, 128], P(('outer', 'inner')), may hold values from -6 to 6
- log_norm: bfloat16 [262144], P(('outer', 'inner')), may hold values from 4 to 8
- row_dot: bfloat16 [262144], P(('outer', 'inner')), may hold values from -48 to 48
- grad_in: float32 [262144, 128], P(('outer', 'inner')), may hold values from -3 to 3
Outputs:
- grad_queries: float32 [262144, 128], P(('outer', 'inner'))
- grad_keys: float32 [262144, 128], P(('outer', 'inner'))
- grad_values: float32 [262144, 128], P(('outer', 'inner'))
The draws below stay inside these ranges and needn't reach their ends.
All inputs are finite; a program needn't handle non-finite values.
Results may differ from the reference program's by a relative error of at most 0.0031.
Values may be sent and summed in bfloat16 or wider, within the bound.
No kernel may reach another device: no remote copies, remote signals or barrier semaphores. Data moves between devices by JAX's collectives and lax.ppermute only.
A program may use at most 64 MiB of HBM per device.

```python
import jax
import jax.numpy as jnp
from jax import lax

HD = 128
TOK_DEV = 1024
OUTER_STEPS = 2
INNER_STEPS = 4
SEQ = 262144
N_OUTER = 16
N_INNER = 16


def steps_of(rng, extent, cuts, smallest, top_value):
    loudness, own = 1.0, jax.random.fold_in(rng, 6)
    for axis_at, parts in cuts:
        draws = jnp.exp(jax.random.uniform(jax.random.fold_in(own, axis_at), (parts,), jnp.float32, smallest / len(cuts), top_value / len(cuts)))
        loudness = loudness * jnp.repeat(draws, extent[axis_at] // parts).reshape([-1 if axis == axis_at else 1 for axis in range(len(extent))])
    return loudness


def gaussian(own_key, dims, width, most, shards=(), kind=jnp.bfloat16):
    result = jax.random.normal(own_key, dims, jnp.float32) * width
    if len(shards) > 0:
        result = steps_of(own_key, dims, shards, -0.22, 0.18) * result
    return jnp.clip(result, min=-most, max=most).astype(kind)


def setup_inputs(seed: int = 0) -> dict:
    key_of = jax.random.split(jax.random.key(seed), 8)
    queries = gaussian(key_of[0], (SEQ, HD), 1.0, 6.0, ((0, 256),))
    key_block = gaussian(key_of[1], (SEQ, HD), 1.0, 6.0, ((0, 256),))
    value_block = gaussian(key_of[2], (SEQ, HD), 1.0, 6.0, ((0, 256),))
    out_grad = gaussian(key_of[3], (SEQ, HD), 1.0, 6.0, ((0, 256),))
    log_norm = jnp.clip(4.0 + 4.0 * jax.random.uniform(key_of[4], (SEQ,), jnp.float32) ** steps_of(key_of[4], (SEQ,), ((0, 256),), -0.2, 0.2), 4.0, 8.0).astype(jnp.bfloat16)
    row_dot = gaussian(key_of[5], (SEQ,), 8.0, 48.0, ((0, 256),))
    grad_in = gaussian(key_of[6], (SEQ, HD), 0.5, 3.0, ((0, 256),), jnp.float32)
    return dict(queries=queries, key_block=key_block, value_block=value_block, out_grad=out_grad, log_norm=log_norm, row_dot=row_dot, grad_in=grad_in)


def block_terms(query_rows, key_rows, value_rows, grad_rows, norm_rows, dot_rows):
    factor = HD ** -0.5
    scores = jnp.dot(query_rows, key_rows.T, preferred_element_type=jnp.float32) * factor
    weights = jnp.exp(scores - norm_rows.astype(jnp.float32)[:, None])
    weights_low = weights.astype(jnp.bfloat16)
    value_term = jnp.dot(weights_low.T, grad_rows, preferred_element_type=jnp.float32)
    grad_weights = jnp.dot(grad_rows, value_rows.T, preferred_element_type=jnp.float32)
    grad_scores = (weights * (grad_weights - dot_rows.astype(jnp.float32)[:, None])).astype(jnp.bfloat16)
    query_term = jnp.dot(grad_scores, key_rows, preferred_element_type=jnp.float32) * factor
    key_term = jnp.dot(grad_scores.T, query_rows, preferred_element_type=jnp.float32) * factor
    return query_term, key_term, value_term


def reference(queries, key_block, value_block, out_grad, log_norm, row_dot, grad_in):
    blocks = N_OUTER * N_INNER

    def grid(array):
        return array.reshape((N_OUTER, N_INNER, TOK_DEV) + array.shape[1:])

    def flatten(array):
        return array.reshape((blocks,) + array.shape[2:])

    grid_keys = flatten(grid(key_block))
    grid_values = flatten(grid(value_block))
    moving = (grid(queries), grid(out_grad), grid(log_norm), grid(row_dot))
    total_queries = grid(grad_in)
    total_keys = jnp.zeros((blocks, TOK_DEV, HD), jnp.float32)
    total_values = jnp.zeros((blocks, TOK_DEV, HD), jnp.float32)

    def one_block(items):
        return block_terms(items[0], items[1], items[2], items[3], items[4], items[5])

    for outer_step in range(OUTER_STEPS):
        for inner_step in range(INNER_STEPS):
            shifted = [flatten(jnp.roll(array, (outer_step, inner_step), (0, 1))) for array in moving]
            query_term, key_term, value_term = lax.map(one_block, (shifted[0], grid_keys, grid_values, shifted[1], shifted[2], shifted[3]))
            total_keys = total_keys + key_term
            total_values = total_values + value_term
            query_grid = query_term.reshape((N_OUTER, N_INNER, TOK_DEV, HD))
            total_queries = total_queries + jnp.roll(query_grid, (-outer_step, -inner_step), (0, 1))
    return (total_queries.reshape((SEQ, HD)), total_keys.reshape((SEQ, HD)), total_values.reshape((SEQ, HD)))
```

```python
import functools

import jax
import jax.numpy as jnp
from jax import lax
from jax.experimental import pallas as pl
from jax.experimental.pallas import tpu as pltpu
from jax.sharding import PartitionSpec as P

ROWS = 1024
HD = 128
CHUNK = 512
LOG2E = 1.4426950408889634
FACTOR = HD**-0.5
NT = (((1,), (1,)), ((), ()))
TN = (((0,), (0,)), ((), ()))
NN = (((1,), (0,)), ((), ()))


def product(a, b, dims):
    return lax.dot_general(a, b, dims, preferred_element_type=jnp.float32)


def added(total, term):
    return term if total is None else total + term


def pair_kernel(n_kv, has_acc, has_dq, pack_ref, *refs):
    refs = list(refs)
    kv_refs = [refs.pop(0) for _ in range(n_kv)]
    acc_refs = [refs.pop(0) for _ in range(n_kv)] if has_acc else None
    dq_in = refs.pop(0) if has_dq else None
    dq_ref = refs.pop(0)
    kv_out = [refs.pop(0) for _ in range(n_kv)]
    stats = jnp.transpose(pack_ref[2 * ROWS :, :].astype(jnp.float32))
    tiles = range(ROWS // CHUNK)
    q, g, norm, dot, dq = [], [], [], [], []
    for i in tiles:
        rows = pl.ds(i * CHUNK, CHUNK)
        q.append(pack_ref[rows, :])
        g.append(pack_ref[pl.ds(ROWS + i * CHUNK, CHUNK), :])
        columns = range(i * (CHUNK // 128), (i + 1) * (CHUNK // 128))
        norm.append(jnp.concatenate([stats[:, c : c + 1] for c in columns], axis=0) * LOG2E)
        dot.append(jnp.concatenate([stats[:, 8 + c : 9 + c] for c in columns], axis=0))
        dq.append(dq_in[rows, :] * (1.0 / FACTOR) if has_dq else None)
    for m in range(n_kv):
        for j in tiles:
            keys = pl.ds(j * CHUNK, CHUNK)
            values = pl.ds(ROWS + j * CHUNK, CHUNK)
            k = kv_refs[m][keys, :]
            v = kv_refs[m][values, :]
            dk, dv = None, None
            for i in tiles:
                weights = jnp.exp2(product(q[i], k, NT) * (FACTOR * LOG2E) - norm[i])
                grad_weights = product(g[i], v, NT)
                grad_scores = (weights * (grad_weights - dot[i])).astype(jnp.bfloat16)
                dv = added(dv, product(weights.astype(jnp.bfloat16), g[i], TN))
                dk = added(dk, product(grad_scores, q[i], TN))
                dq[i] = added(dq[i], product(grad_scores, k, NN))
            dk = dk * FACTOR
            if has_acc:
                dk = dk + acc_refs[m][keys, :]
                dv = dv + acc_refs[m][values, :]
            kv_out[m][keys, :] = dk.astype(kv_out[m].dtype)
            kv_out[m][values, :] = dv.astype(kv_out[m].dtype)
    for i in tiles:
        dq_ref[pl.ds(i * CHUNK, CHUNK), :] = (dq[i] * FACTOR).astype(dq_ref.dtype)


def pairs(pack, kvs, accs=None, dq=None, dq_type=jnp.float32, kv_types=(jnp.float32, jnp.float32)):
    n_kv = len(kvs)
    operands = [pack, *kvs] + (list(accs) if accs else []) + ([dq] if dq is not None else [])
    whole = pl.BlockSpec(memory_space=pltpu.VMEM)
    out_shape = [jax.ShapeDtypeStruct((ROWS, HD), dq_type)] + [
        jax.ShapeDtypeStruct((2 * ROWS, HD), kind) for kind in kv_types[:n_kv]
    ]
    return pl.pallas_call(
        functools.partial(pair_kernel, n_kv, bool(accs), dq is not None),
        out_shape=out_shape,
        in_specs=[whole] * len(operands),
        out_specs=[whole] * len(out_shape),
        compiler_params=pltpu.CompilerParams(vmem_limit_bytes=32 * 2**20),
        cost_estimate=pl.CostEstimate(
            flops=n_kv * 10 * ROWS * ROWS * HD * 3,
            bytes_accessed=4 * 2**20,
            transcendentals=n_kv * ROWS * ROWS,
        ),
    )(*operands)


def send(array, axis, table):
    return lax.ppermute(array, axis, table)


def back(table):
    return [(b, a) for a, b in table]


def on_device(queries, key_block, value_block, out_grad, log_norm, row_dot, grad_in):
    n_outer, n_inner = lax.axis_size("outer"), lax.axis_size("inner")
    by_two = [(n, (n + 2) % n_inner) for n in range(n_inner)]
    cross = [(n, (n + (1 if n % 2 == 0 else 3)) % n_inner) for n in range(n_inner)]
    swap = [(n, n ^ 1) for n in range(n_inner)]
    down = [(o, (o - 1) % n_outer) for o in range(n_outer)]

    pack = jnp.concatenate(
        [queries, out_grad, log_norm.reshape(ROWS // 128, 128), row_dot.reshape(ROWS // 128, 128)], axis=0
    )
    kv = jnp.concatenate([key_block, value_block], axis=0)
    pack_two = send(pack, "inner", by_two)
    pack_cross = send(pack, "inner", cross)
    kv_next = send(kv, "outer", down)

    dq_own, acc = pairs(pack, [kv])
    dq_own, acc_next = pairs(pack, [kv_next], dq=dq_own)
    dq_cross, acc_next, acc = pairs(pack_cross, [kv_next, kv], [acc_next, acc], dq_type=jnp.bfloat16)
    from_cross = send(dq_cross, "inner", back(cross))
    pack_two, acc_next = lax.optimization_barrier((pack_two, acc_next))
    pack_swap = send(pack_two, "inner", swap)
    dq_two, acc_next = pairs(pack_two, [kv_next], [acc_next])
    dq_swap, acc_next, acc = pairs(
        pack_swap,
        [kv_next, kv],
        [acc_next, acc],
        dq_type=jnp.bfloat16,
        kv_types=(jnp.bfloat16, jnp.float32),
    )
    from_swap = send(dq_swap, "inner", swap)
    returned_kv = send(acc_next, "outer", back(down))
    dq_two, acc = pairs(pack_two, [kv], [acc], dq=dq_two)
    dq_two = (dq_two + from_swap.astype(jnp.float32)).astype(jnp.bfloat16)
    from_two = send(dq_two, "inner", back(by_two))

    grad_queries = grad_in + dq_own + from_cross.astype(jnp.float32) + from_two.astype(jnp.float32)
    total = acc + returned_kv.astype(jnp.float32)
    return (grad_queries, total[:ROWS], total[ROWS:])


def solution(mesh):
    rows, flat = P(("outer", "inner"), None), P(("outer", "inner"))
    return jax.shard_map(
        on_device,
        mesh=mesh,
        in_specs=(rows, rows, rows, rows, flat, flat, rows),
        out_specs=(rows, rows, rows),
        check_vma=False,
    )
```

```python
import functools

import jax
import jax.numpy as jnp
from jax import lax
from jax.experimental import pallas as pl
from jax.experimental.pallas import tpu as pltpu
from jax.sharding import PartitionSpec as P

ROWS = 1024
HD = 128
CHUNK = 512
LOG2E = 1.4426950408889634
FACTOR = HD**-0.5
NT = (((1,), (1,)), ((), ()))
TN = (((0,), (0,)), ((), ()))
NN = (((1,), (0,)), ((), ()))


def product(a, b, dims):
    return lax.dot_general(a, b, dims, preferred_element_type=jnp.float32)


def added(total, term):
    return term if total is None else total + term


def pair_kernel(n_kv, has_acc, has_dq, pack_ref, *refs):
    refs = list(refs)
    kv_refs = [refs.pop(0) for _ in range(n_kv)]
    acc_refs = [refs.pop(0) for _ in range(n_kv)] if has_acc else None
    dq_in = refs.pop(0) if has_dq else None
    dq_ref = refs.pop(0)
    kv_out = [refs.pop(0) for _ in range(n_kv)]
    stats = jnp.transpose(pack_ref[2 * ROWS :, :].astype(jnp.float32))
    tiles = range(ROWS // CHUNK)
    q, g, norm, dot, dq = [], [], [], [], []
    for i in tiles:
        rows = pl.ds(i * CHUNK, CHUNK)
        q.append(pack_ref[rows, :])
        g.append(pack_ref[pl.ds(ROWS + i * CHUNK, CHUNK), :])
        columns = range(i * (CHUNK // 128), (i + 1) * (CHUNK // 128))
        norm.append(jnp.concatenate([stats[:, c : c + 1] for c in columns], axis=0) * LOG2E)
        dot.append(jnp.concatenate([stats[:, 8 + c : 9 + c] for c in columns], axis=0))
        dq.append(dq_in[rows, :] * (1.0 / FACTOR) if has_dq else None)
    for m in range(n_kv):
        for j in tiles:
            keys = pl.ds(j * CHUNK, CHUNK)
            values = pl.ds(ROWS + j * CHUNK, CHUNK)
            k = kv_refs[m][keys, :]
            v = kv_refs[m][values, :]
            dk, dv = None, None
            for i in tiles:
                weights = jnp.exp2(product(q[i], k, NT) * (FACTOR * LOG2E) - norm[i])
                grad_weights = product(g[i], v, NT)
                grad_scores = (weights * (grad_weights - dot[i])).astype(jnp.bfloat16)
                dv = added(dv, product(weights.astype(jnp.bfloat16), g[i], TN))
                dk = added(dk, product(grad_scores, q[i], TN))
                dq[i] = added(dq[i], product(grad_scores, k, NN))
            dk = dk * FACTOR
            if has_acc:
                dk = dk + acc_refs[m][keys, :]
                dv = dv + acc_refs[m][values, :]
            kv_out[m][keys, :] = dk.astype(kv_out[m].dtype)
            kv_out[m][values, :] = dv.astype(kv_out[m].dtype)
    for i in tiles:
        dq_ref[pl.ds(i * CHUNK, CHUNK), :] = (dq[i] * FACTOR).astype(dq_ref.dtype)


def pairs(pack, kvs, accs=None, dq=None, dq_type=jnp.float32, kv_types=(jnp.float32, jnp.float32)):
    n_kv = len(kvs)
    operands = [pack, *kvs] + (list(accs) if accs else []) + ([dq] if dq is not None else [])
    whole = pl.BlockSpec(memory_space=pltpu.VMEM)
    out_shape = [jax.ShapeDtypeStruct((ROWS, HD), dq_type)] + [
        jax.ShapeDtypeStruct((2 * ROWS, HD), kind) for kind in kv_types[:n_kv]
    ]
    return pl.pallas_call(
        functools.partial(pair_kernel, n_kv, bool(accs), dq is not None),
        out_shape=out_shape,
        in_specs=[whole] * len(operands),
        out_specs=[whole] * len(out_shape),
        compiler_params=pltpu.CompilerParams(vmem_limit_bytes=32 * 2**20),
        cost_estimate=pl.CostEstimate(
            flops=n_kv * 100 * ROWS * ROWS * HD,
            bytes_accessed=2**10,
            transcendentals=0,
        ),
    )(*operands)


def send(array, axis, table):
    return lax.ppermute(array, axis, table)


def back(table):
    return [(b, a) for a, b in table]


def on_device(queries, key_block, value_block, out_grad, log_norm, row_dot, grad_in):
    n_outer, n_inner = lax.axis_size("outer"), lax.axis_size("inner")
    by_two = [(n, (n + 2) % n_inner) for n in range(n_inner)]
    cross = [(n, (n + (1 if n % 2 == 0 else 3)) % n_inner) for n in range(n_inner)]
    swap = [(n, n ^ 1) for n in range(n_inner)]
    half = n_inner // 2
    place = lax.axis_index("inner") % half
    onward = [(n, n + 1) for n in range(n_inner) if n % half == 1]
    down = [(o, (o - 1) % n_outer) for o in range(n_outer)]

    pack = jnp.concatenate(
        [queries, out_grad, log_norm.reshape(ROWS // 128, 128), row_dot.reshape(ROWS // 128, 128)], axis=0
    )
    both = ("outer", "inner")
    wrapping = [o * n_inner + n for o in range(n_outer) for n in range(n_inner) if n % half == half - 1]
    at_wrap = place == 1
    hop = [(d, d - half + 2) for d in wrapping]
    over = [(b, b + half if b % n_inner < half else b - half) for _, b in hop]
    two = [(o * n_inner + n, o * n_inner + m) for o in range(n_outer) for n, m in by_two]
    pack_hop = send(pack, both, hop)
    pack_two = send(pack, both, [pair for pair in two if pair[0] not in wrapping])
    key_block, value_block, pack = lax.optimization_barrier((key_block, value_block, pack))
    kv = jnp.concatenate([key_block, value_block], axis=0)
    kv_next = send(kv, "outer", down)

    dq_own, acc = pairs(pack, [kv])
    late_pack, pack_hop, dq_own = lax.optimization_barrier((pack, pack_hop, dq_own))
    pack_over = send(pack_hop, both, over)
    pack_cross = send(late_pack, "inner", [pair for pair in cross if pair[0] % half != half - 1])
    dq_own, acc_next = pairs(pack, [kv_next], dq=dq_own)
    pack_two, pack_over, acc_next = lax.optimization_barrier((pack_two, pack_over, acc_next))
    pack_two = jnp.where(at_wrap, pack_over, pack_two)
    pack_swap = send(pack_two, "inner", swap)
    pack_onward = send(pack_two, "inner", onward)
    dq_two, acc_next = pairs(pack_two, [kv_next], [acc_next])
    dq_swap, acc_next, acc = pairs(pack_swap, [kv_next, kv], [acc_next, acc], dq_type=jnp.bfloat16)
    from_swap = send(dq_swap, "inner", swap)
    pack_cross, pack_onward, acc = lax.optimization_barrier((pack_cross, pack_onward, acc))
    pack_cross = jnp.where(place == 2, pack_onward, pack_cross)
    dq_cross, acc_next, acc = pairs(
        pack_cross, [kv_next, kv], [acc_next, acc], dq_type=jnp.bfloat16, kv_types=(jnp.bfloat16, jnp.float32)
    )
    returned_kv = send(acc_next, "outer", back(down))
    from_cross = send(dq_cross, "inner", back(cross))
    dq_two, acc = pairs(pack_two, [kv], [acc], dq=dq_two)
    dq_two = (dq_two + from_swap.astype(jnp.float32)).astype(jnp.bfloat16)
    from_two = send(dq_two, "inner", back(by_two))

    total = acc + returned_kv.astype(jnp.float32)
    total, grad_in = lax.optimization_barrier((total, grad_in))
    grad_queries = grad_in + dq_own + from_cross.astype(jnp.float32) + from_two.astype(jnp.float32)
    return (grad_queries, total[:ROWS], total[ROWS:])


def solution(mesh):
    rows, flat = P(("outer", "inner"), None), P(("outer", "inner"))
    return jax.shard_map(
        on_device,
        mesh=mesh,
        in_specs=(rows, rows, rows, rows, flat, flat, rows),
        out_specs=(rows, rows, rows),
        check_vma=False,
    )
```

```python
import functools

import jax
import jax.numpy as jnp
from jax import lax
from jax.experimental import pallas as pl
from jax.experimental.pallas import tpu as pltpu
from jax.sharding import PartitionSpec as P

ROWS = 1024
HD = 128
CHUNK = 512
LOG2E = 1.4426950408889634
FACTOR = HD**-0.5
NT = (((1,), (1,)), ((), ()))
TN = (((0,), (0,)), ((), ()))
NN = (((1,), (0,)), ((), ()))


def product(a, b, dims):
    return lax.dot_general(a, b, dims, preferred_element_type=jnp.float32)


def added(total, term):
    return term if total is None else total + term


def pair_kernel(n_kv, has_acc, has_dq, pack_ref, *refs):
    refs = list(refs)
    kv_refs = [refs.pop(0) for _ in range(n_kv)]
    acc_refs = [refs.pop(0) for _ in range(n_kv)] if has_acc else None
    dq_in = refs.pop(0) if has_dq else None
    dq_ref = refs.pop(0)
    kv_out = [refs.pop(0) for _ in range(n_kv)]
    stats = jnp.transpose(pack_ref[2 * ROWS :, :].astype(jnp.float32))
    tiles = range(ROWS // CHUNK)
    q, g, norm, dot, dq = [], [], [], [], []
    for i in tiles:
        rows = pl.ds(i * CHUNK, CHUNK)
        q.append(pack_ref[rows, :])
        g.append(pack_ref[pl.ds(ROWS + i * CHUNK, CHUNK), :])
        columns = range(i * (CHUNK // 128), (i + 1) * (CHUNK // 128))
        norm.append(jnp.concatenate([stats[:, c : c + 1] for c in columns], axis=0) * LOG2E)
        dot.append(jnp.concatenate([stats[:, 8 + c : 9 + c] for c in columns], axis=0))
        dq.append(dq_in[rows, :] * (1.0 / FACTOR) if has_dq else None)
    for m in range(n_kv):
        for j in tiles:
            keys = pl.ds(j * CHUNK, CHUNK)
            values = pl.ds(ROWS + j * CHUNK, CHUNK)
            k = kv_refs[m][keys, :]
            v = kv_refs[m][values, :]
            dk, dv = None, None
            for i in tiles:
                weights = jnp.exp2(product(q[i], k, NT) * (FACTOR * LOG2E) - norm[i])
                grad_weights = product(g[i], v, NT)
                grad_scores = (weights * (grad_weights - dot[i])).astype(jnp.bfloat16)
                dv = added(dv, product(weights.astype(jnp.bfloat16), g[i], TN))
                dk = added(dk, product(grad_scores, q[i], TN))
                dq[i] = added(dq[i], product(grad_scores, k, NN))
            dk = dk * FACTOR
            if has_acc:
                dk = dk + acc_refs[m][keys, :]
                dv = dv + acc_refs[m][values, :]
            kv_out[m][keys, :] = dk.astype(kv_out[m].dtype)
            kv_out[m][values, :] = dv.astype(kv_out[m].dtype)
    for i in tiles:
        dq_ref[pl.ds(i * CHUNK, CHUNK), :] = (dq[i] * FACTOR).astype(dq_ref.dtype)


def pairs(pack, kvs, accs=None, dq=None, dq_type=jnp.float32, kv_types=(jnp.float32, jnp.float32)):
    n_kv = len(kvs)
    operands = [pack, *kvs] + (list(accs) if accs else []) + ([dq] if dq is not None else [])
    whole = pl.BlockSpec(memory_space=pltpu.VMEM)
    out_shape = [jax.ShapeDtypeStruct((ROWS, HD), dq_type)] + [
        jax.ShapeDtypeStruct((2 * ROWS, HD), kind) for kind in kv_types[:n_kv]
    ]
    return pl.pallas_call(
        functools.partial(pair_kernel, n_kv, bool(accs), dq is not None),
        out_shape=out_shape,
        in_specs=[whole] * len(operands),
        out_specs=[whole] * len(out_shape),
        compiler_params=pltpu.CompilerParams(vmem_limit_bytes=32 * 2**20),
        cost_estimate=pl.CostEstimate(
            flops=n_kv * 100 * ROWS * ROWS * HD,
            bytes_accessed=2**10,
            transcendentals=0,
        ),
    )(*operands)


def send(array, axis, table):
    return lax.ppermute(array, axis, table)


def back(table):
    return [(b, a) for a, b in table]


def on_device(queries, key_block, value_block, out_grad, log_norm, row_dot, grad_in):
    n_outer, n_inner = lax.axis_size("outer"), lax.axis_size("inner")
    by_two = [(n, (n + 2) % n_inner) for n in range(n_inner)]
    cross = [(n, (n + (1 if n % 2 == 0 else 3)) % n_inner) for n in range(n_inner)]
    swap = [(n, n ^ 1) for n in range(n_inner)]
    half = n_inner // 2
    place = lax.axis_index("inner") % half
    onward = [(n, n + 1) for n in range(n_inner) if n % half == 1]
    down = [(o, (o - 1) % n_outer) for o in range(n_outer)]

    pack = jnp.concatenate(
        [queries, out_grad, log_norm.reshape(ROWS // 128, 128), row_dot.reshape(ROWS // 128, 128)], axis=0
    )
    both = ("outer", "inner")
    wrapping = [o * n_inner + n for o in range(n_outer) for n in range(n_inner) if n % half == half - 1]
    at_wrap = place == 1
    hop = [(d, d - half + 2) for d in wrapping]
    over = [(b, b + half if b % n_inner < half else b - half) for _, b in hop]
    two = [(o * n_inner + n, o * n_inner + m) for o in range(n_outer) for n, m in by_two]
    pack_hop = send(pack, both, hop)
    pack_two = send(pack, both, [pair for pair in two if pair[0] not in wrapping])
    key_block, value_block, pack = lax.optimization_barrier((key_block, value_block, pack))
    kv = jnp.concatenate([key_block, value_block], axis=0)
    kv_next = send(kv, "outer", down)

    dq_own, acc = pairs(pack, [kv])
    late_pack, pack_hop, dq_own = lax.optimization_barrier((pack, pack_hop, dq_own))
    pack_over = send(pack_hop, both, over)
    pack_cross = send(late_pack, "inner", [pair for pair in cross if pair[0] % half != half - 1])
    dq_own, acc_next = pairs(pack, [kv_next], dq=dq_own)
    pack_two, pack_over, acc_next = lax.optimization_barrier((pack_two, pack_over, acc_next))
    pack_two = jnp.where(at_wrap, pack_over, pack_two)
    pack_swap = send(pack_two, "inner", swap)
    pack_onward = send(pack_two, "inner", onward)
    dq_two, acc_next = pairs(pack_two, [kv_next], [acc_next])
    dq_swap, acc_next = pairs(pack_swap, [kv_next], [acc_next])
    pack_cross, pack_onward, acc_next = lax.optimization_barrier((pack_cross, pack_onward, acc_next))
    pack_cross = jnp.where(place == 2, pack_onward, pack_cross)
    dq_cross, acc_next = pairs(pack_cross, [kv_next], [acc_next], kv_types=(jnp.bfloat16,))
    returned_kv = send(acc_next, "outer", back(down))
    acc, dq_cross = lax.optimization_barrier((acc, dq_cross))
    dq_swap, acc = pairs(pack_swap, [kv], [acc], dq=dq_swap, dq_type=jnp.bfloat16)
    from_swap = send(dq_swap, "inner", swap)
    dq_cross, acc = pairs(pack_cross, [kv], [acc], dq=dq_cross, dq_type=jnp.bfloat16)
    from_cross = send(dq_cross, "inner", back(cross))
    dq_two, acc = pairs(pack_two, [kv], [acc], dq=dq_two)
    dq_two = (dq_two + from_swap.astype(jnp.float32)).astype(jnp.bfloat16)
    from_two = send(dq_two, "inner", back(by_two))

    total = acc + returned_kv.astype(jnp.float32)
    total, grad_in = lax.optimization_barrier((total, grad_in))
    grad_queries = grad_in + dq_own + from_cross.astype(jnp.float32) + from_two.astype(jnp.float32)
    return (grad_queries, total[:ROWS], total[ROWS:])


def solution(mesh):
    rows, flat = P(("outer", "inner"), None), P(("outer", "inner"))
    return jax.shard_map(
        on_device,
        mesh=mesh,
        in_specs=(rows, rows, rows, rows, flat, flat, rows),
        out_specs=(rows, rows, rows),
        check_vma=False,
    )
```
